32 devices in a mesh: expert: 8 (over z, y), rep: 4 (over x, core).
Axes of the slice: x: 2, y: 2, z: 4, core: 2. Of those that a mesh axis runs over, the one named last changes fastest.
Arguments:
- tokens: bfloat16 [1024, 1024], P('expert', 'rep'), may hold values from -6 to 6
- cotangent: bfloat16 [1024, 1024], P('expert', 'rep'), may hold values from -1.796875 to 1.796875
- expert_ids: int32 [1024, 2], P('expert'), may hold values from 0 to 7, all different within a row; in each aligned block of 128 rows (0 to 127, 128 to 255, ...) at most 64 rows name the same one
- gate_values: float32 [1024, 2], P('expert'), may hold values from 0.1 to 0.9
- inner_weight: bfloat16 [8, 1024, 4096], P('expert', None, 'rep'), may hold values from -0.1875 to 0.1875
- outer_weight: bfloat16 [8, 4096, 1024], P('expert', 'rep'), may hold values from -0.09375 to 0.09375
Outputs:
- output: bfloat16 [1024, 1024], P('expert', 'rep')
- input_grads: bfloat16 [1024, 1024], P('expert', 'rep')
- gate_grads: float32 [1024, 2], P('expert')
The draws below stay inside these ranges and needn't reach their ends.
Inputs may be any that keep to these rules, and one draw needn't show every extreme that they name: `expert_ids`: each token names 2 different experts. Among the 128 tokens of one block no expert is named more than 64 times, a bound that some block reaches.
All inputs are finite; a program needn't handle non-finite values.
Results may differ from the reference program's by a relative error of at most 0.012.
Values may be sent and summed in bfloat16 or wider, within the bound.
A program may use at most 64 MiB of HBM per device.

```python
import math
import jax
import jax.numpy as jnp
import numpy as np
from jax import lax

D = 1024
EXPERTS = 8
TOP = 2
FF_W = 4096
TOK = 128
CAP = 64
TOKENS = 1024
N_REP = 4


def levels(stream_key, extent, pieces, low, top_value):
    loudness = 1.0
    for dim, shards_of in pieces:
        draws = jax.random.uniform(jax.random.fold_in(jax.random.fold_in(stream_key, 6), dim), (shards_of,), jnp.float32, low / len(pieces), top_value / len(pieces))
        loudness = loudness * jnp.repeat(jnp.exp(draws), extent[dim] // shards_of).reshape((-1,) + (1,) * (len(extent) - 1 - dim))
    return loudness


def assign_block(stream_key, own, number, rows, number_of, top, reach, skew):
    order = jax.random.permutation(stream_key, number_of)
    heavy_load, usual = portions_of(number_of, rows * top, reach, skew, True), portions_of(number_of, rows * top, reach, skew, False)
    places = jnp.arange(number_of)

    def named(lengths, rotation):
        used = int((lengths > 0).sum())
        fixed = max(1, used // 4)
        passed = fixed + (places - fixed + rotation * (used - fixed)) % max(1, number_of - fixed)
        return jnp.zeros((number_of,), jnp.int32).at[order[jnp.where(places < fixed, places, passed)]].set(jnp.asarray(lengths, jnp.int32))

    lengths = jnp.where(number % 4 == 0, named(heavy_load, number // 4), named(usual, number - number // 4 - 1))
    mixed = jax.random.permutation(jax.random.fold_in(own, 3), number_of)
    giver, receiver = mixed[0:number_of // 2 * 2:2], mixed[1:number_of // 2 * 2:2]
    room = jnp.minimum(lengths[giver] - 1, reach - lengths[receiver]) // 2
    room = jnp.where((giver == order[0]) | (receiver == order[0]) | (lengths[receiver] == 0), 0, jnp.maximum(room, 0))
    passed = jax.random.randint(jax.random.fold_in(own, 4), (number_of // 2,), 0, 1 << 20) % (room + 1)
    lengths = lengths.at[giver].add(-passed).at[receiver].add(passed)
    members = jnp.searchsorted(jnp.cumsum(lengths), jnp.arange(rows * top), side="right").astype(jnp.int32)
    grid = members.reshape(top, rows).T
    grid = grid[jax.random.permutation(jax.random.fold_in(own, 1), rows)]
    rotation = jax.random.randint(jax.random.fold_in(own, 2), (rows, 1), 0, top)
    return jnp.take_along_axis(grid, (jnp.arange(top)[None, :] + rotation) % top, axis=1)


def portions_of(number_of, total, limit, slope, full):
    weights = [(1 << 20) // math.isqrt(standing ** slope) + 1 for standing in range(1, number_of + 1)]
    largest = limit if full else min(limit, max(-(-total // number_of), total * weights[0] // sum(weights)))
    least = 1 if total - largest >= number_of - 1 else 0
    counts, rest = [largest] + [least] * (number_of - 1), total - largest - least * (number_of - 1)
    while rest > 0:
        free = [i for i in range(1, number_of) if counts[i] < largest] or [i for i in range(1, number_of) if counts[i] < limit]
        mass, remaining = sum([weights[i] for i in free]), rest
        for i in free:
            more = min(limit - counts[i], max(1, remaining * weights[i] // mass), rest)
            counts[i] = counts[i] + more
            rest = rest - more
    return np.array(counts)


def normal_values(rng, extent, spread, limit, shards=(), kind=jnp.bfloat16):
    level = levels(rng, extent, shards, -0.22, 0.18) if shards else 1.0
    entries = jax.random.normal(rng, extent, jnp.float32) * spread * level
    return jnp.minimum(jnp.maximum(entries, -limit), limit).astype(kind)


def setup_inputs(seed: int = 0) -> dict:
    splits = jax.random.split(jax.random.key(seed), 7)
    tokens = normal_values(splits[0], (TOKENS, D), 1.0, 6.0, ((0, 8), (1, 4)))
    cotangent = normal_values(splits[1], (TOKENS, D), 0.3, 1.796875, ((0, 8), (1, 4)))
    expert_ids_keys = jax.random.split(jax.random.fold_in(splits[2], 1), TOKENS // TOK)
    expert_ids_turns = jax.random.permutation(jax.random.fold_in(splits[2], 3), TOKENS // TOK)
    expert_ids = jax.vmap(lambda own, number: assign_block(jax.random.fold_in(splits[2], 2), own, number, TOK, EXPERTS, TOP, CAP, 2))(expert_ids_keys, expert_ids_turns).reshape((TOKENS, TOP))
    gate_values = jnp.clip(0.1 + 0.79999997 * jax.random.uniform(splits[3], (TOKENS, TOP), jnp.float32) ** levels(splits[3], (TOKENS, TOP), ((0, 8),), -0.2, 0.2), 0.1, 0.9)
    inner_weight = normal_values(splits[4], (EXPERTS, D, FF_W), D ** -0.5, 0.1875, ((0, 8), (2, 4)))
    outer_weight = normal_values(splits[5], (EXPERTS, FF_W, D), FF_W ** -0.5, 0.09375, ((0, 8), (1, 4)))
    return dict(tokens=tokens, cotangent=cotangent, expert_ids=expert_ids, gate_values=gate_values, inner_weight=inner_weight, outer_weight=outer_weight)


SQRT_TWO_PI = 0.7978845608028654
CUBIC = 0.044715


def gelu_pair(preact):
    argument = SQRT_TWO_PI * (preact + CUBIC * preact * preact * preact)
    tangent = jnp.tanh(argument)
    result = 0.5 * preact * (1.0 + tangent)
    derivative = 0.5 * (1.0 + tangent) + 0.5 * preact * (1.0 - tangent * tangent) * SQRT_TWO_PI * (1.0 + 3.0 * CUBIC * preact * preact)
    return result, derivative


def grouped_out(hidden, outer):
    group = FF_W // N_REP
    total = jnp.zeros((hidden.shape[0], outer.shape[1]), jnp.float32)
    for part in range(N_REP):
        piece = jnp.dot(hidden[:, part * group:(part + 1) * group], outer[part * group:(part + 1) * group, :], preferred_element_type=jnp.float32)
        total = total + piece.astype(jnp.bfloat16).astype(jnp.float32)
    return total.astype(jnp.bfloat16)


def grouped_in(back_pre, inner):
    group = FF_W // N_REP
    total = jnp.zeros((back_pre.shape[0], inner.shape[0]), jnp.float32)
    for part in range(N_REP):
        piece = lax.dot_general(back_pre[:, part * group:(part + 1) * group], inner[:, part * group:(part + 1) * group], (((1,), (1,)), ((), ())), preferred_element_type=jnp.float32)
        total = total + piece.astype(jnp.bfloat16).astype(jnp.float32)
    return total.astype(jnp.bfloat16)


def reference(tokens, cotangent, expert_ids, gate_values, inner_weight, outer_weight):
    blocks = TOKENS // TOK
    assigns = TOK * TOP
    block_ids = expert_ids.reshape(blocks, assigns).astype(jnp.int32)
    matches = (block_ids[:, :, None] == jnp.arange(EXPERTS, dtype=jnp.int32)[None, None, :]).astype(jnp.int32)
    ranked = jnp.sum((jnp.cumsum(matches, axis=1) - 1) * matches, axis=2).astype(jnp.int32)
    position = (block_ids * blocks + jnp.arange(blocks, dtype=jnp.int32)[:, None]) * CAP + ranked
    owners = jnp.full((EXPERTS * blocks * CAP,), -1, dtype=jnp.int32)
    owners = owners.at[position.reshape(-1)].set(jnp.arange(TOKENS * TOP, dtype=jnp.int32))
    owners = owners.reshape(EXPERTS, blocks * CAP)
    flat_gates = gate_values.reshape(-1)

    def per_expert(carry, inputs):
        out_store, in_store = carry
        owner_row, inner, outer = inputs
        valid = owner_row >= 0
        safe = jnp.where(valid, owner_row, 0).astype(jnp.int32)
        token_index = (safe // TOP).astype(jnp.int32)
        expert_rows = jnp.where(valid[:, None], tokens[token_index], jnp.zeros((), tokens.dtype))
        gate_here = jnp.where(valid, flat_gates[safe], jnp.zeros((), flat_gates.dtype))
        expert_grads = (gate_here[:, None] * cotangent[token_index].astype(jnp.float32)).astype(jnp.bfloat16)
        preact = jnp.dot(expert_rows, inner, preferred_element_type=jnp.float32)
        result, derivative = gelu_pair(preact)
        hidden = result.astype(jnp.bfloat16)
        expert_out = grouped_out(hidden, outer)
        back_hidden = lax.dot_general(expert_grads, outer, (((1,), (1,)), ((), ())), preferred_element_type=jnp.float32)
        back_pre = (back_hidden * derivative).astype(jnp.bfloat16)
        slot_input = grouped_in(back_pre, inner)
        target = jnp.where(valid, owner_row, TOKENS * TOP).astype(jnp.int32)
        out_store = out_store.at[target].set(expert_out, mode="drop")
        in_store = in_store.at[target].set(slot_input, mode="drop")
        return (out_store, in_store), None

    start_store = (jnp.zeros((TOKENS * TOP, D), jnp.bfloat16), jnp.zeros((TOKENS * TOP, D), jnp.bfloat16))
    (out_store, in_store), unused = lax.scan(per_expert, start_store, (owners, inner_weight, outer_weight))
    out_store = out_store.reshape(TOKENS, TOP, D)
    in_store = in_store.reshape(TOKENS, TOP, D)
    cot_wide = cotangent.astype(jnp.float32)
    combined = jnp.zeros((TOKENS, D), jnp.float32)
    in_total = jnp.zeros((TOKENS, D), jnp.float32)
    columns = []
    for member in range(TOP):
        picked = out_store[:, member, :].astype(jnp.float32)
        combined = combined + gate_values[:, member:member + 1] * picked
        columns.append(jnp.sum(cot_wide * picked, axis=1))
        in_total = in_total + in_store[:, member, :].astype(jnp.float32)
    output = combined.astype(jnp.bfloat16)
    input_grads = in_total.astype(jnp.bfloat16)
    gate_grads = jnp.stack(columns, axis=1)
    return output, input_grads, gate_grads
```

```python
import jax
import jax.numpy as jnp
from jax import lax
from jax.experimental import pallas as pl
from jax.experimental.pallas import tpu as pltpu
from jax.sharding import PartitionSpec as P

TOP = 2


SQRT_TWO_PI = 0.7978845608028654
CUBIC = 0.044715


def gelu_pair(preact):
    argument = SQRT_TWO_PI * (preact + CUBIC * preact * preact * preact)
    tangent = jnp.tanh(argument)
    result = 0.5 * preact * (1.0 + tangent)
    derivative = 0.5 * (1.0 + tangent) + 0.5 * preact * (1.0 - tangent * tangent) * SQRT_TWO_PI * (
        1.0 + 3.0 * CUBIC * preact * preact
    )
    return (result, derivative)


def slot_tables(expert_ids, experts, capacity):
    flat_ids = expert_ids.reshape(-1)
    matches = (flat_ids[:, None] == jnp.arange(experts, dtype=jnp.int32)[None, :]).astype(jnp.bfloat16)
    order = jnp.arange(flat_ids.shape[0], dtype=jnp.int32)
    earlier = (order[None, :] < order[:, None]).astype(jnp.bfloat16)
    counts = jnp.dot(earlier, matches, preferred_element_type=jnp.float32)
    ranked = jnp.sum(counts * matches.astype(jnp.float32), axis=1).astype(jnp.int32)
    target = (flat_ids * capacity + ranked).reshape(expert_ids.shape[0], expert_ids.shape[1]).T
    slot_index = jnp.arange(experts * capacity, dtype=jnp.int32)
    return (slot_index[None, :, None] == target[:, None, :]).astype(jnp.bfloat16)


def build_slots(slot_table, gate_values, token_part, cot_part):
    slot_rows = jnp.dot(
        jnp.sum(slot_table, axis=0), token_part, preferred_element_type=jnp.float32
    ).astype(jnp.bfloat16)
    cot_float = cot_part.astype(jnp.float32)
    grad_acc = jnp.zeros((slot_table.shape[1], token_part.shape[1]), jnp.float32)
    for member in range(TOP):
        scaled = (gate_values[:, member : member + 1] * cot_float).astype(jnp.bfloat16)
        grad_acc = grad_acc + jnp.dot(
            slot_table[member], scaled, preferred_element_type=jnp.float32
        )
    return (slot_rows, grad_acc.astype(jnp.bfloat16))


def per_device_xla(tokens, cotangent, expert_ids, gate_values, inner_weight, outer_weight):
    quarter = tokens.shape[1]
    experts = lax.axis_size("expert") * inner_weight.shape[0]
    capacity = 2 * tokens.shape[0] * TOP // experts
    slot_table = slot_tables(expert_ids, experts, capacity)
    cot_wide = cotangent.astype(jnp.float32)
    slot_rows, slot_grads = build_slots(slot_table, gate_values, tokens, cotangent)
    part_rows, part_grads = (
        lax.all_to_all(
            slot_rows.reshape(experts, capacity, quarter),
            "expert",
            split_axis=0,
            concat_axis=0,
            tiled=True,
        ),
        lax.all_to_all(
            slot_grads.reshape(experts, capacity, quarter),
            "expert",
            split_axis=0,
            concat_axis=0,
            tiled=True,
        ),
    )
    arrived_rows, arrived_grads = (
        lax.all_gather(part_rows, "rep", axis=2, tiled=True),
        lax.all_gather(part_grads, "rep", axis=2, tiled=True),
    )
    feature_width = arrived_rows.shape[2]
    expert_rows = arrived_rows.reshape(-1, feature_width)
    expert_grads = arrived_grads.reshape(-1, feature_width)
    slot_count = expert_rows.shape[0]
    inner_block = inner_weight[0]
    outer_block = outer_weight[0]
    preact = jnp.dot(expert_rows, inner_block, preferred_element_type=jnp.float32)
    result, derivative = gelu_pair(preact)
    hidden = result.astype(jnp.bfloat16)
    back_hidden = lax.dot_general(
        expert_grads, outer_block, (((1,), (1,)), ((), ())), preferred_element_type=jnp.float32
    )
    back_pre = (back_hidden * derivative).astype(jnp.bfloat16)
    term_out = lax.dot_general(
        outer_block, hidden, (((0,), (1,)), ((), ())), preferred_element_type=jnp.float32
    )
    term_in = lax.dot_general(
        inner_block, back_pre, (((1,), (1,)), ((), ())), preferred_element_type=jnp.float32
    )
    joined = jnp.concatenate([term_out, term_in], axis=1)
    summed = lax.psum_scatter(
        joined.astype(jnp.bfloat16).astype(jnp.float32).astype(jnp.bfloat16),
        "rep",
        scatter_dimension=0,
        tiled=True,
    ).astype(jnp.float32)
    expert_out = summed[:, :slot_count].T.astype(jnp.bfloat16)
    slot_input = summed[:, slot_count:].T.astype(jnp.bfloat16)
    back_out, back_input = (
        lax.all_to_all(
            expert_out.reshape(-1, capacity, quarter),
            "expert",
            split_axis=0,
            concat_axis=0,
            tiled=True,
        ),
        lax.all_to_all(
            slot_input.reshape(-1, capacity, quarter),
            "expert",
            split_axis=0,
            concat_axis=0,
            tiled=True,
        ),
    )
    back_out = back_out.reshape(-1, quarter)
    back_input = back_input.reshape(-1, quarter)
    combined = jnp.zeros((tokens.shape[0], quarter), jnp.float32)
    in_total = jnp.zeros((tokens.shape[0], quarter), jnp.float32)
    columns = []
    for member in range(TOP):
        picked = lax.dot_general(
            slot_table[member],
            back_out,
            (((0,), (0,)), ((), ())),
            preferred_element_type=jnp.float32,
        )
        combined = combined + gate_values[:, member : member + 1] * picked
        columns.append(jnp.sum(cot_wide * picked, axis=1))
        in_total = in_total + lax.dot_general(
            slot_table[member],
            back_input,
            (((0,), (0,)), ((), ())),
            preferred_element_type=jnp.float32,
        )
    output = combined.astype(jnp.bfloat16)
    input_grads = in_total.astype(jnp.bfloat16)
    gate_grads = lax.psum(jnp.stack(columns, axis=1), "rep")
    return (output, input_grads, gate_grads)


MESH = pl.DeviceIdType.MESH
GROUP = 2


def flip(index, bits):
    step = 1
    result = index
    while step <= bits:
        if bits & step:
            result = result + step * (1 - 2 * lax.rem(lax.div(index, step), 2))
        step *= 2
    return result


def kernel(
    ids, gates, tokens, cotangent, inner_any, outer_any,
    output, input_grads, gate_grads,
    inner, outer, sent, arrived, square, hidden, back_pre, own,
    core_out, core_in, chip_out, chip_in, back_sent, back_in, gate_out, gate_in,
    weight_sem, a2a_send, a2a_recv, gather_send, gather_recv, core_send, core_recv,
    chip_send, chip_recv, back_send, back_recv, gate_send, gate_recv,
):
    experts, _, capacity, quarter = sent.shape
    rows = tokens.shape[0]
    reps = arrived.shape[0]
    units = outer.shape[0]
    chunks = experts // GROUP
    span = GROUP * capacity
    me, part = lax.axis_index("expert"), lax.axis_index("rep")

    def to_expert(j):
        return (flip(me, j), part)

    def to_rep(q):
        return (me, flip(part, q))

    barrier = pltpu.get_barrier_semaphore()
    for j in range(1, experts):
        pl.semaphore_signal(barrier, inc=1, device_id=to_expert(j), device_id_type=MESH)
    for q in range(1, reps):
        pl.semaphore_signal(barrier, inc=1, device_id=to_rep(q), device_id_type=MESH)

    loads = []
    for q in range(reps):
        start = pl.multiple_of(flip(part, q) * quarter, quarter)
        here = pl.ds(q * quarter, quarter)
        loads.append(pltpu.make_async_copy(inner_any.at[pl.ds(start, quarter), :], inner.at[here, :], weight_sem.at[0, q]))
        loads.append(pltpu.make_async_copy(outer_any.at[:, pl.ds(start, quarter)], outer.at[:, here], weight_sem.at[1, q]))
    for load in loads:
        load.start()

    padded = max(experts, 16)
    expert_iota = lax.broadcasted_iota(jnp.int32, (padded, rows), 0)
    match = [jnp.where(expert_iota == ids[k : k + 1, :], 1.0, 0.0) for k in range(TOP)]
    before = lax.broadcasted_iota(jnp.int32, (rows, rows), 0) < lax.broadcasted_iota(jnp.int32, (rows, rows), 1)
    prior = jnp.dot(
        (match[0] + match[1]).astype(jnp.bfloat16),
        jnp.where(before, 1.0, 0.0).astype(jnp.bfloat16),
        preferred_element_type=jnp.float32,
    )
    targets = []
    for k in range(TOP):
        rank = jnp.sum(prior * match[k], axis=0, keepdims=True).astype(jnp.int32)
        targets.append((ids[k : k + 1, :] ^ me) * capacity + rank)
    slot_iota = lax.broadcasted_iota(jnp.int32, (experts * capacity, rows), 0)
    table = [jnp.where(slot_iota == targets[k], 1.0, 0.0).astype(jnp.bfloat16) for k in range(TOP)]
    square[...] = jnp.zeros_like(square)
    for k in range(TOP):
        square[k : k + 1, :] = targets[k].astype(jnp.float32)
        square[TOP + k : TOP + k + 1, :] = gates[k : k + 1, :]
    columns = square[...].T
    gate_columns = [columns[:, TOP + k : TOP + k + 1] for k in range(TOP)]
    cot = cotangent[...].astype(jnp.float32)
    slot_rows = jnp.dot(table[0] + table[1], tokens[...], preferred_element_type=jnp.float32).astype(jnp.bfloat16)
    slot_grads = jnp.dot(
        table[0], (gate_columns[0] * cot).astype(jnp.bfloat16), preferred_element_type=jnp.float32
    ) + jnp.dot(table[1], (gate_columns[1] * cot).astype(jnp.bfloat16), preferred_element_type=jnp.float32)
    slot_grads = slot_grads.astype(jnp.bfloat16)
    for j in range(experts):
        target = arrived.at[0, 0] if j == 0 else sent.at[j]
        target[0] = slot_rows[j * capacity : (j + 1) * capacity, :]
        target[1] = slot_grads[j * capacity : (j + 1) * capacity, :]

    def remote(source, target, send, recv, device):
        return pltpu.make_async_remote_copy(
            src_ref=source, dst_ref=target, send_sem=send, recv_sem=recv, device_id=device, device_id_type=MESH
        )

    dispatch = {
        j: remote(sent.at[j], arrived.at[0, j], a2a_send.at[j], a2a_recv.at[j], to_expert(j))
        for j in range(1, experts)
    }
    gather = {
        (g, j): remote(arrived.at[a, j], arrived.at[b, j], gather_send.at[g, j], gather_recv.at[g, j], to_rep(hop))
        for g, (a, b, hop) in enumerate(((0, 1, 1), (0, 2, 2), (2, 3, 1)))
        for j in range(experts)
    }
    core = [remote(core_out.at[c], core_in.at[c], core_send.at[c], core_recv.at[c], to_rep(1)) for c in range(chunks)]
    chip = [remote(chip_out.at[c], chip_in.at[c], chip_send.at[c], chip_recv.at[c], to_rep(2)) for c in range(chunks)]
    back = {
        j: remote(back_sent.at[j], back_in.at[j], back_send.at[j], back_recv.at[j], to_expert(j))
        for j in range(1, experts)
    }
    gate = [remote(gate_out, gate_in.at[q], gate_send.at[q], gate_recv.at[q], to_rep(q)) for q in range(1, reps)]

    pl.semaphore_wait(barrier, experts - 1 + reps - 1)

    def members(c):
        return range(c * GROUP, (c + 1) * GROUP)

    def step_a(c):
        for j in members(c):
            if j:
                dispatch[j].wait_recv()
            gather[1, j].start()
            gather[0, j].start()

    def step_b(c):
        for j in members(c):
            gather[1, j].wait_recv()
            gather[2, j].start()

    def step_c(c):
        for j in members(c):
            gather[0, j].wait_recv()
            gather[2, j].wait_recv()
        if c == 0:
            for load in loads:
                load.wait()

        def operand(kind):
            return jnp.concatenate(
                [jnp.concatenate([arrived[q, j, kind] for q in range(reps)], axis=1) for j in members(c)], axis=0
            )

        expert_rows, expert_grads = operand(0), operand(1)
        tile = min(units, 256)
        for h in range(units // tile):
            at = slice(h * tile, (h + 1) * tile)
            preact = jnp.dot(expert_rows, inner[:, at], preferred_element_type=jnp.float32)
            spread = lax.dot_general(
                expert_grads, outer[at, :], (((1,), (1,)), ((), ())), preferred_element_type=jnp.float32
            )
            result, derivative = gelu_pair(preact)
            hidden[:, at] = result.astype(jnp.bfloat16)
            back_pre[:, at] = (spread * derivative).astype(jnp.bfloat16)
        for q in (1, 3, 0, 2):
            at = slice(q * quarter, (q + 1) * quarter)
            term_out = jnp.dot(hidden[...], outer[:, at], preferred_element_type=jnp.float32)
            term_in = lax.dot_general(
                back_pre[...], inner[at, :], (((1,), (1,)), ((), ())), preferred_element_type=jnp.float32
            )
            if q % 2:
                core_out[c, q // 2, 0] = term_out.astype(jnp.bfloat16)
                core_out[c, q // 2, 1] = term_in.astype(jnp.bfloat16)
                if q == 3:
                    core[c].start()
            else:
                own[c, q // 2, 0] = term_out
                own[c, q // 2, 1] = term_in

    def step_d(c):
        core[c].wait_recv()
        chip_out[c] = (own[c, 1] + core_in[c, 1].astype(jnp.float32)).astype(jnp.bfloat16)
        chip[c].start()
        own[c, 0] = own[c, 0] + core_in[c, 0].astype(jnp.float32)

    def step_e(c):
        chip[c].wait_recv()
        total = (own[c, 0] + chip_in[c].astype(jnp.float32)).astype(jnp.bfloat16)
        for i, j in enumerate(members(c)):
            target = back_sent.at[j] if j else back_in.at[0]
            target[...] = total[:, i * capacity : (i + 1) * capacity, :]
            if j:
                back[j].start()

    for j in send_order(experts):
        dispatch[j].start()
    steps = dict(a=step_a, b=step_b, c=step_c, d=step_d, e=step_e)
    for name, c in schedule(chunks):
        steps[name](c)

    lane_iota = lax.broadcasted_iota(jnp.int32, (rows, span), 1).astype(jnp.float32)
    picked = [jnp.zeros((rows, quarter), jnp.float32) for _ in range(TOP)]
    in_total = jnp.zeros((rows, quarter), jnp.float32)
    for c in range(chunks):
        for j in members(c):
            if j:
                back[j].wait_recv()
        slots = [
            jnp.where(lane_iota + float(c * span) == columns[:, k : k + 1], 1.0, 0.0).astype(jnp.bfloat16)
            for k in range(TOP)
        ]
        outs, ins = (jnp.concatenate([back_in[j, kind] for j in members(c)], axis=0) for kind in range(2))
        for k in range(TOP):
            picked[k] = picked[k] + jnp.dot(slots[k], outs, preferred_element_type=jnp.float32)
        in_total = in_total + jnp.dot(slots[0] + slots[1], ins, preferred_element_type=jnp.float32)
    lane = lax.broadcasted_iota(jnp.int32, (rows, square.shape[1]), 1)
    sums = jnp.zeros(square.shape, jnp.float32)
    for k in range(TOP):
        sums = jnp.where(lane == k, jnp.sum(cot * picked[k], axis=1, keepdims=True), sums)
    gate_out[...] = sums.T[: gate_out.shape[0], :]
    for copy in gate:
        copy.start()
    output[...] = (gate_columns[0] * picked[0] + gate_columns[1] * picked[1]).astype(jnp.bfloat16)
    input_grads[...] = in_total.astype(jnp.bfloat16)
    for copy in (*dispatch.values(), *gather.values(), *core, *chip, *back.values()):
        copy.wait_send()
    for copy in gate:
        copy.wait()
    total = (gate_out[...] + gate_in[1]) + (gate_in[2] + gate_in[3])
    gate_grads[...] = total[:TOP, :]


def send_order(experts):
    half = experts // 2
    near, far = list(range(1, half)), list(range(half, experts))
    order = []
    while near or far:
        if near:
            order.append(near.pop(0))
        if far:
            order.append(far.pop(0))
    return order


def schedule(chunks):
    plan = []
    for s in range(chunks + 4):
        for name, lag in (("a", 0), ("b", 1), ("e", 4), ("d", 3), ("c", 2)):
            if 0 <= s - lag < chunks:
                plan.append((name, s - lag))
    return plan


def per_device(tokens, cotangent, expert_ids, gate_values, inner_weight, outer_weight):
    rows, quarter = tokens.shape
    experts, reps = lax.axis_size("expert"), lax.axis_size("rep")
    capacity = 2 * rows * TOP // experts
    width, units = inner_weight.shape[1:]
    fits = (
        inner_weight.shape[0] == 1 and reps == 4 and capacity % 16 == 0 and rows % 128 == 0 and quarter % 128 == 0
        and units % 256 == 0 and experts & (experts - 1) == 0 and experts % GROUP == 0
    )
    if not fits:
        return per_device_xla(tokens, cotangent, expert_ids, gate_values, inner_weight, outer_weight)
    chunks, span = experts // GROUP, GROUP * capacity
    half, dma = jnp.bfloat16, pltpu.SemaphoreType.DMA
    output, input_grads, gate_grads = pl.pallas_call(
        kernel,
        out_shape=(
            jax.ShapeDtypeStruct((rows, quarter), half),
            jax.ShapeDtypeStruct((rows, quarter), half),
            jax.ShapeDtypeStruct((TOP, rows), jnp.float32),
        ),
        in_specs=[pl.BlockSpec(memory_space=pltpu.VMEM)] * 4 + [pl.BlockSpec(memory_space=pl.ANY)] * 2,
        out_specs=[pl.BlockSpec(memory_space=pltpu.VMEM)] * 3,
        scratch_shapes=[
            pltpu.VMEM((width, units), half),
            pltpu.VMEM((units, width), half),
            pltpu.VMEM((experts, 2, capacity, quarter), half),
            pltpu.VMEM((reps, experts, 2, capacity, quarter), half),
            pltpu.VMEM((rows, rows), jnp.float32),
            pltpu.VMEM((span, units), half),
            pltpu.VMEM((span, units), half),
            pltpu.VMEM((chunks, 2, 2, span, quarter), jnp.float32),
            pltpu.VMEM((chunks, 2, 2, span, quarter), half),
            pltpu.VMEM((chunks, 2, 2, span, quarter), half),
            pltpu.VMEM((chunks, 2, span, quarter), half),
            pltpu.VMEM((chunks, 2, span, quarter), half),
            pltpu.VMEM((experts, 2, capacity, quarter), half),
            pltpu.VMEM((experts, 2, capacity, quarter), half),
            pltpu.VMEM((8, rows), jnp.float32),
            pltpu.VMEM((reps, 8, rows), jnp.float32),
            dma((2, reps)), dma((experts,)), dma((experts,)), dma((3, experts)), dma((3, experts)),
            dma((chunks,)), dma((chunks,)), dma((chunks,)), dma((chunks,)),
            dma((experts,)), dma((experts,)), dma((reps,)), dma((reps,)),
        ],
        compiler_params=pltpu.CompilerParams(
            collective_id=0, has_side_effects=True, vmem_limit_bytes=56 * 2**20
        ),
    )(expert_ids.T, gate_values.T, tokens, cotangent, inner_weight[0], outer_weight[0])
    return (output, input_grads, gate_grads.T)


def solution(mesh):
    placed = (
        P("expert", "rep"),
        P("expert", "rep"),
        P("expert", None),
        P("expert", None),
        P("expert", None, "rep"),
        P("expert", "rep", None),
    )
    return jax.shard_map(
        per_device,
        mesh=mesh,
        in_specs=placed,
        out_specs=(P("expert", "rep"), P("expert", "rep"), P("expert", None)),
        check_vma=False,
    )
```

```python
import jax
import jax.numpy as jnp
from jax import lax
from jax.experimental import pallas as pl
from jax.experimental.pallas import tpu as pltpu
from jax.sharding import PartitionSpec as P

TOP = 2


SQRT_TWO_PI = 0.7978845608028654
CUBIC = 0.044715


def gelu_pair(preact):
    argument = SQRT_TWO_PI * (preact + CUBIC * preact * preact * preact)
    tangent = jnp.tanh(argument)
    result = 0.5 * preact * (1.0 + tangent)
    derivative = 0.5 * (1.0 + tangent) + 0.5 * preact * (1.0 - tangent * tangent) * SQRT_TWO_PI * (
        1.0 + 3.0 * CUBIC * preact * preact
    )
    return (result, derivative)


def slot_tables(expert_ids, experts, capacity):
    flat_ids = expert_ids.reshape(-1)
    matches = (flat_ids[:, None] == jnp.arange(experts, dtype=jnp.int32)[None, :]).astype(jnp.bfloat16)
    order = jnp.arange(flat_ids.shape[0], dtype=jnp.int32)
    earlier = (order[None, :] < order[:, None]).astype(jnp.bfloat16)
    counts = jnp.dot(earlier, matches, preferred_element_type=jnp.float32)
    ranked = jnp.sum(counts * matches.astype(jnp.float32), axis=1).astype(jnp.int32)
    target = (flat_ids * capacity + ranked).reshape(expert_ids.shape[0], expert_ids.shape[1]).T
    slot_index = jnp.arange(experts * capacity, dtype=jnp.int32)
    return (slot_index[None, :, None] == target[:, None, :]).astype(jnp.bfloat16)


def build_slots(slot_table, gate_values, token_part, cot_part):
    slot_rows = jnp.dot(
        jnp.sum(slot_table, axis=0), token_part, preferred_element_type=jnp.float32
    ).astype(jnp.bfloat16)
    cot_float = cot_part.astype(jnp.float32)
    grad_acc = jnp.zeros((slot_table.shape[1], token_part.shape[1]), jnp.float32)
    for member in range(TOP):
        scaled = (gate_values[:, member : member + 1] * cot_float).astype(jnp.bfloat16)
        grad_acc = grad_acc + jnp.dot(
            slot_table[member], scaled, preferred_element_type=jnp.float32
        )
    return (slot_rows, grad_acc.astype(jnp.bfloat16))


def per_device_xla(tokens, cotangent, expert_ids, gate_values, inner_weight, outer_weight):
    quarter = tokens.shape[1]
    experts = lax.axis_size("expert") * inner_weight.shape[0]
    capacity = 2 * tokens.shape[0] * TOP // experts
    slot_table = slot_tables(expert_ids, experts, capacity)
    cot_wide = cotangent.astype(jnp.float32)
    slot_rows, slot_grads = build_slots(slot_table, gate_values, tokens, cotangent)
    part_rows, part_grads = (
        lax.all_to_all(
            slot_rows.reshape(experts, capacity, quarter),
            "expert",
            split_axis=0,
            concat_axis=0,
            tiled=True,
        ),
        lax.all_to_all(
            slot_grads.reshape(experts, capacity, quarter),
            "expert",
            split_axis=0,
            concat_axis=0,
            tiled=True,
        ),
    )
    arrived_rows, arrived_grads = (
        lax.all_gather(part_rows, "rep", axis=2, tiled=True),
        lax.all_gather(part_grads, "rep", axis=2, tiled=True),
    )
    feature_width = arrived_rows.shape[2]
    expert_rows = arrived_rows.reshape(-1, feature_width)
    expert_grads = arrived_grads.reshape(-1, feature_width)
    slot_count = expert_rows.shape[0]
    inner_block = inner_weight[0]
    outer_block = outer_weight[0]
    preact = jnp.dot(expert_rows, inner_block, preferred_element_type=jnp.float32)
    result, derivative = gelu_pair(preact)
    hidden = result.astype(jnp.bfloat16)
    back_hidden = lax.dot_general(
        expert_grads, outer_block, (((1,), (1,)), ((), ())), preferred_element_type=jnp.float32
    )
    back_pre = (back_hidden * derivative).astype(jnp.bfloat16)
    term_out = lax.dot_general(
        outer_block, hidden, (((0,), (1,)), ((), ())), preferred_element_type=jnp.float32
    )
    term_in = lax.dot_general(
        inner_block, back_pre, (((1,), (1,)), ((), ())), preferred_element_type=jnp.float32
    )
    joined = jnp.concatenate([term_out, term_in], axis=1)
    summed = lax.psum_scatter(
        joined.astype(jnp.bfloat16).astype(jnp.float32).astype(jnp.bfloat16),
        "rep",
        scatter_dimension=0,
        tiled=True,
    ).astype(jnp.float32)
    expert_out = summed[:, :slot_count].T.astype(jnp.bfloat16)
    slot_input = summed[:, slot_count:].T.astype(jnp.bfloat16)
    back_out, back_input = (
        lax.all_to_all(
            expert_out.reshape(-1, capacity, quarter),
            "expert",
            split_axis=0,
            concat_axis=0,
            tiled=True,
        ),
        lax.all_to_all(
            slot_input.reshape(-1, capacity, quarter),
            "expert",
            split_axis=0,
            concat_axis=0,
            tiled=True,
        ),
    )
    back_out = back_out.reshape(-1, quarter)
    back_input = back_input.reshape(-1, quarter)
    combined = jnp.zeros((tokens.shape[0], quarter), jnp.float32)
    in_total = jnp.zeros((tokens.shape[0], quarter), jnp.float32)
    columns = []
    for member in range(TOP):
        picked = lax.dot_general(
            slot_table[member],
            back_out,
            (((0,), (0,)), ((), ())),
            preferred_element_type=jnp.float32,
        )
        combined = combined + gate_values[:, member : member + 1] * picked
        columns.append(jnp.sum(cot_wide * picked, axis=1))
        in_total = in_total + lax.dot_general(
            slot_table[member],
            back_input,
            (((0,), (0,)), ((), ())),
            preferred_element_type=jnp.float32,
        )
    output = combined.astype(jnp.bfloat16)
    input_grads = in_total.astype(jnp.bfloat16)
    gate_grads = lax.psum(jnp.stack(columns, axis=1), "rep")
    return (output, input_grads, gate_grads)


MESH = pl.DeviceIdType.MESH
GROUP = 2


def flip(index, bits):
    step = 1
    result = index
    while step <= bits:
        if bits & step:
            result = result + step * (1 - 2 * lax.rem(lax.div(index, step), 2))
        step *= 2
    return result


def kernel(
    ids, gates, tokens, cotangent, inner_any, outer_any,
    output, input_grads, gate_grads,
    inner, outer, sent, arrived, square, hidden, back_pre, own,
    core_out, core_in, chip_out, chip_in, back_sent, back_in, gate_out, gate_in,
    weight_sem, a2a_send, a2a_recv, gather_send, gather_recv, core_send, core_recv,
    chip_send, chip_recv, back_send, back_recv, gate_send, gate_recv,
):
    experts, _, capacity, quarter = sent.shape
    rows = tokens.shape[0]
    reps = arrived.shape[0]
    units = outer.shape[0]
    chunks = experts // GROUP
    span = GROUP * capacity
    me, part = lax.axis_index("expert"), lax.axis_index("rep")

    def to_expert(j):
        return (flip(me, j), part)

    def to_rep(q):
        return (me, flip(part, q))

    barrier = pltpu.get_barrier_semaphore()
    for j in range(1, experts):
        pl.semaphore_signal(barrier, inc=1, device_id=to_expert(j), device_id_type=MESH)
    for q in range(1, reps):
        pl.semaphore_signal(barrier, inc=1, device_id=to_rep(q), device_id_type=MESH)

    loads = []
    for q in range(reps):
        start = pl.multiple_of(flip(part, q) * quarter, quarter)
        here = pl.ds(q * quarter, quarter)
        loads.append(pltpu.make_async_copy(inner_any.at[pl.ds(start, quarter), :], inner.at[here, :], weight_sem.at[0, q]))
        loads.append(pltpu.make_async_copy(outer_any.at[:, pl.ds(start, quarter)], outer.at[:, here], weight_sem.at[1, q]))
    for load in loads:
        load.start()

    padded = max(experts, 16)
    expert_iota = lax.broadcasted_iota(jnp.int32, (padded, rows), 0)
    match = [jnp.where(expert_iota == ids[k : k + 1, :], 1.0, 0.0) for k in range(TOP)]
    before = lax.broadcasted_iota(jnp.int32, (rows, rows), 0) < lax.broadcasted_iota(jnp.int32, (rows, rows), 1)
    prior = jnp.dot(
        (match[0] + match[1]).astype(jnp.bfloat16),
        jnp.where(before, 1.0, 0.0).astype(jnp.bfloat16),
        preferred_element_type=jnp.float32,
    )
    targets = []
    for k in range(TOP):
        rank = jnp.sum(prior * match[k], axis=0, keepdims=True).astype(jnp.int32)
        targets.append((ids[k : k + 1, :] ^ me) * capacity + rank)
    slot_iota = lax.broadcasted_iota(jnp.int32, (experts * capacity, rows), 0)
    table = [jnp.where(slot_iota == targets[k], 1.0, 0.0).astype(jnp.bfloat16) for k in range(TOP)]
    square[...] = jnp.zeros_like(square)
    for k in range(TOP):
        square[k : k + 1, :] = targets[k].astype(jnp.float32)
        square[TOP + k : TOP + k + 1, :] = gates[k : k + 1, :]
    columns = square[...].T
    gate_columns = [columns[:, TOP + k : TOP + k + 1] for k in range(TOP)]
    cot = cotangent[...].astype(jnp.float32)
    slot_rows = jnp.dot(table[0] + table[1], tokens[...], preferred_element_type=jnp.float32).astype(jnp.bfloat16)
    slot_grads = jnp.dot(
        table[0], (gate_columns[0] * cot).astype(jnp.bfloat16), preferred_element_type=jnp.float32
    ) + jnp.dot(table[1], (gate_columns[1] * cot).astype(jnp.bfloat16), preferred_element_type=jnp.float32)
    slot_grads = slot_grads.astype(jnp.bfloat16)
    for j in range(experts):
        target = arrived.at[0, 0] if j == 0 else sent.at[j]
        target[0] = slot_rows[j * capacity : (j + 1) * capacity, :]
        target[1] = slot_grads[j * capacity : (j + 1) * capacity, :]

    def remote(source, target, send, recv, device):
        return pltpu.make_async_remote_copy(
            src_ref=source, dst_ref=target, send_sem=send, recv_sem=recv, device_id=device, device_id_type=MESH
        )

    dispatch = {
        j: remote(sent.at[j], arrived.at[0, j], a2a_send.at[j], a2a_recv.at[j], to_expert(j))
        for j in range(1, experts)
    }
    gather = {
        (g, j): remote(arrived.at[a, j], arrived.at[b, j], gather_send.at[g, j], gather_recv.at[g, j], to_rep(hop))
        for g, (a, b, hop) in enumerate(((0, 1, 1), (0, 2, 2), (2, 3, 1)))
        for j in range(experts)
    }
    core = {
        (c, i): remote(core_out.at[c, i], core_in.at[c, i], core_send.at[c, i], core_recv.at[c, i], to_rep(1))
        for c in range(chunks)
        for i in range(2)
    }
    chip = [remote(chip_out.at[c], chip_in.at[c], chip_send.at[c], chip_recv.at[c], to_rep(2)) for c in range(chunks)]
    back = {
        j: remote(back_sent.at[j], back_in.at[j], back_send.at[j], back_recv.at[j], to_expert(j))
        for j in range(1, experts)
    }
    gate = [remote(gate_out, gate_in.at[q], gate_send.at[q], gate_recv.at[q], to_rep(q)) for q in range(1, reps)]

    pl.semaphore_wait(barrier, experts - 1 + reps - 1)

    def members(c):
        return range(c * GROUP, (c + 1) * GROUP)

    def step_a(c):
        for j in members(c):
            if j:
                dispatch[j].wait_recv()
            gather[1, j].start()
            gather[0, j].start()

    def step_b(c):
        for j in members(c):
            gather[1, j].wait_recv()
            gather[2, j].start()

    def step_c(c):
        for j in members(c):
            gather[0, j].wait_recv()
            gather[2, j].wait_recv()
        if c == chunk_order(chunks)[0]:
            for load in loads:
                load.wait()

        def operand(kind):
            return jnp.concatenate(
                [jnp.concatenate([arrived[q, j, kind] for q in range(reps)], axis=1) for j in members(c)], axis=0
            )

        expert_rows, expert_grads = operand(0), operand(1)
        tile = min(units, 256)
        for h in range(units // tile):
            at = slice(h * tile, (h + 1) * tile)
            preact = jnp.dot(expert_rows, inner[:, at], preferred_element_type=jnp.float32)
            spread = lax.dot_general(
                expert_grads, outer[at, :], (((1,), (1,)), ((), ())), preferred_element_type=jnp.float32
            )
            result, derivative = gelu_pair(preact)
            hidden[:, at] = result.astype(jnp.bfloat16)
            back_pre[:, at] = (spread * derivative).astype(jnp.bfloat16)

    def step_o(c):
        for q in (3, 2, 1, 0):
            at = slice(q * quarter, (q + 1) * quarter)
            term_out = jnp.dot(hidden[...], outer[:, at], preferred_element_type=jnp.float32)
            term_in = lax.dot_general(
                back_pre[...], inner[at, :], (((1,), (1,)), ((), ())), preferred_element_type=jnp.float32
            )
            if q % 2:
                core_out[c, q // 2, 0] = term_out.astype(jnp.bfloat16)
                core_out[c, q // 2, 1] = term_in.astype(jnp.bfloat16)
                core[c, q // 2].start()
            else:
                own[c, q // 2, 0] = term_out
                own[c, q // 2, 1] = term_in

    def step_d(c):
        core[c, 1].wait_recv()
        chip_out[c] = (own[c, 1] + core_in[c, 1].astype(jnp.float32)).astype(jnp.bfloat16)
        chip[c].start()

    def step_e(c):
        core[c, 0].wait_recv()
        chip[c].wait_recv()
        total = (own[c, 0] + core_in[c, 0].astype(jnp.float32) + chip_in[c].astype(jnp.float32)).astype(jnp.bfloat16)
        for i, j in enumerate(members(c)):
            target = back_sent.at[j] if j else back_in.at[0]
            target[...] = total[:, i * capacity : (i + 1) * capacity, :]
            if j:
                back[j].start()

    for j in send_order(experts):
        dispatch[j].start()
    steps = dict(a=step_a, b=step_b, c=step_c, o=step_o, d=step_d, e=step_e)
    for name, c in schedule(chunks):
        steps[name](c)

    lane_iota = lax.broadcasted_iota(jnp.int32, (rows, span), 1).astype(jnp.float32)
    picked = [jnp.zeros((rows, quarter), jnp.float32) for _ in range(TOP)]
    in_total = jnp.zeros((rows, quarter), jnp.float32)
    for c in chunk_order(chunks):
        for j in members(c):
            if j:
                back[j].wait_recv()
        slots = [
            jnp.where(lane_iota + float(c * span) == columns[:, k : k + 1], 1.0, 0.0).astype(jnp.bfloat16)
            for k in range(TOP)
        ]
        outs, ins = (jnp.concatenate([back_in[j, kind] for j in members(c)], axis=0) for kind in range(2))
        for k in range(TOP):
            picked[k] = picked[k] + jnp.dot(slots[k], outs, preferred_element_type=jnp.float32)
        in_total = in_total + jnp.dot(slots[0] + slots[1], ins, preferred_element_type=jnp.float32)
    lane = lax.broadcasted_iota(jnp.int32, (rows, square.shape[1]), 1)
    sums = jnp.zeros(square.shape, jnp.float32)
    for k in range(TOP):
        sums = jnp.where(lane == k, jnp.sum(cot * picked[k], axis=1, keepdims=True), sums)
    gate_out[...] = sums.T[: gate_out.shape[0], :]
    for copy in gate:
        copy.start()
    output[...] = (gate_columns[0] * picked[0] + gate_columns[1] * picked[1]).astype(jnp.bfloat16)
    input_grads[...] = in_total.astype(jnp.bfloat16)
    for copy in (*dispatch.values(), *gather.values(), *core.values(), *chip, *back.values()):
        copy.wait_send()
    for copy in gate:
        copy.wait()
    total = (gate_out[...] + gate_in[1]) + (gate_in[2] + gate_in[3])
    gate_grads[...] = total[:TOP, :]


def send_order(experts):
    half = experts // 2
    near, far = list(range(1, half)), list(range(half, experts))
    order = []
    while near or far:
        if near:
            order.append(near.pop(0))
        if far:
            order.append(far.pop(0))
    return order


def chunk_order(chunks):
    near, far = list(range(chunks // 2)), list(range(chunks // 2, chunks))
    return near[:1] + far + near[1:]


def schedule(chunks):
    plan = []
    for s in range(chunks + 4):
        for name, lag in (("a", 0), ("c", 2), ("b", 1), ("e", 4), ("d", 3), ("o", 2)):
            if 0 <= s - lag < chunks:
                plan.append((name, chunk_order(chunks)[s - lag]))
    return plan


def per_device(tokens, cotangent, expert_ids, gate_values, inner_weight, outer_weight):
    rows, quarter = tokens.shape
    experts, reps = lax.axis_size("expert"), lax.axis_size("rep")
    capacity = 2 * rows * TOP // experts
    width, units = inner_weight.shape[1:]
    fits = (
        inner_weight.shape[0] == 1 and reps == 4 and capacity % 16 == 0 and rows % 128 == 0 and quarter % 128 == 0
        and units % 256 == 0 and experts & (experts - 1) == 0 and experts % GROUP == 0
    )
    if not fits:
        return per_device_xla(tokens, cotangent, expert_ids, gate_values, inner_weight, outer_weight)
    chunks, span = experts // GROUP, GROUP * capacity
    half, dma = jnp.bfloat16, pltpu.SemaphoreType.DMA
    output, input_grads, gate_grads = pl.pallas_call(
        kernel,
        out_shape=(
            jax.ShapeDtypeStruct((rows, quarter), half),
            jax.ShapeDtypeStruct((rows, quarter), half),
            jax.ShapeDtypeStruct((TOP, rows), jnp.float32),
        ),
        in_specs=[pl.BlockSpec(memory_space=pltpu.VMEM)] * 4 + [pl.BlockSpec(memory_space=pl.ANY)] * 2,
        out_specs=[pl.BlockSpec(memory_space=pltpu.VMEM)] * 3,
        scratch_shapes=[
            pltpu.VMEM((width, units), half),
            pltpu.VMEM((units, width), half),
            pltpu.VMEM((experts, 2, capacity, quarter), half),
            pltpu.VMEM((reps, experts, 2, capacity, quarter), half),
            pltpu.VMEM((rows, rows), jnp.float32),
            pltpu.VMEM((span, units), half),
            pltpu.VMEM((span, units), half),
            pltpu.VMEM((chunks, 2, 2, span, quarter), jnp.float32),
            pltpu.VMEM((chunks, 2, 2, span, quarter), half),
            pltpu.VMEM((chunks, 2, 2, span, quarter), half),
            pltpu.VMEM((chunks, 2, span, quarter), half),
            pltpu.VMEM((chunks, 2, span, quarter), half),
            pltpu.VMEM((experts, 2, capacity, quarter), half),
            pltpu.VMEM((experts, 2, capacity, quarter), half),
            pltpu.VMEM((8, rows), jnp.float32),
            pltpu.VMEM((reps, 8, rows), jnp.float32),
            dma((2, reps)), dma((experts,)), dma((experts,)), dma((3, experts)), dma((3, experts)),
            dma((chunks, 2)), dma((chunks, 2)), dma((chunks,)), dma((chunks,)),
            dma((experts,)), dma((experts,)), dma((reps,)), dma((reps,)),
        ],
        compiler_params=pltpu.CompilerParams(
            collective_id=0, has_side_effects=True, vmem_limit_bytes=56 * 2**20
        ),
    )(expert_ids.T, gate_values.T, tokens, cotangent, inner_weight[0], outer_weight[0])
    return (output, input_grads, gate_grads.T)


def solution(mesh):
    placed = (
        P("expert", "rep"),
        P("expert", "rep"),
        P("expert", None),
        P("expert", None),
        P("expert", None, "rep"),
        P("expert", "rep", None),
    )
    return jax.shard_map(
        per_device,
        mesh=mesh,
        in_specs=placed,
        out_specs=(P("expert", "rep"), P("expert", "rep"), P("expert", None)),
        check_vma=False,
    )
```
